32 devices in a mesh: rows: 8 (over z, x), cols: 4 (over y, core).
Axes of the slice: x: 2, y: 2, z: 4, core: 2. Of those that a mesh axis runs over, the one named last changes fastest.
Arguments:
- hidden_acts: bfloat16 [1, 27648, 2560], P(None, 'rows'), may hold values from -17 to 17
- out_grads: bfloat16 [1, 2560, 5120], P(None, None, 'cols'), may hold values from -13 to 13
- row_signs: int32 [27648], P('rows'), may hold values from -1 to 1, as said below
- kept_index: int32 [16384], P('rows'), may hold values from 0 to 32767, as said below
Outputs:
- sketch: float32 [1, 16384, 5120], P(None, 'rows', 'cols')
The draws below stay inside these ranges and needn't reach their ends.
Inputs may be any that keep to these rules, and one draw needn't show every extreme that they name: `row_signs`: each entry is +1 or -1. `kept_index`: for each b and each s = 0 .. 7, entries b * 2048 + s * 256 to b * 2048 + (s + 1) * 256 - 1 are distinct padded rows within b * 4096 + s * 512 to b * 4096 + (s + 1) * 512 - 1.
All inputs are finite; a program needn't handle non-finite values.
Results may differ from the reference program's by a relative error of at most 0.0003.
Values sent between devices are 32-bit elements; how exact they have to be, the bound alone decides.
A program may use at most 128 MiB of HBM per device.

```python
import jax
import jax.numpy as jnp
from jax import lax

D = 5120
FF = 27648
PADDED = 32768
KEPT = 16384
TOKENS = 2560
EXAMPLES = 1
PAD_DEV = 4096
KEEP_DEV = 2048
N_ROWS = 8
N_COLS = 4


def draw_hidden_acts(key, part):
    first, second = jax.random.split(jax.random.fold_in(key, 11), 2)
    position = jnp.arange(FF, dtype=jnp.float32) / FF
    level = 0.5 * position + 0.5 * jax.random.uniform(first, (FF,), jnp.float32)
    row_scale = 10.0 ** level
    base = jnp.clip(jax.random.normal(second, (EXAMPLES, FF, TOKENS), jnp.float32), -5.0, 5.0)
    return (base * row_scale[None, :, None] / 3.0).astype(jnp.bfloat16)


def draw_out_grads(key, part):
    first, second = jax.random.split(jax.random.fold_in(key, 23), 2)
    col_scale = 10.0 ** jax.random.uniform(first, (D,), jnp.float32)
    base = jnp.clip(jax.random.normal(second, (EXAMPLES, TOKENS, D), jnp.float32), -5.0, 5.0)
    return (base * col_scale[None, None, :] / 4.0).astype(jnp.bfloat16)


def draw_row_signs(key, part):
    coins = jax.random.randint(jax.random.fold_in(key, 37), (FF,), 0, 2, dtype=jnp.int32)
    return (2 * coins - 1).astype(jnp.int32)


def draw_kept_index(key, part):
    blocks = PADDED // PAD_DEV
    segment = PAD_DEV // N_ROWS
    share = KEEP_DEV // N_ROWS
    keys = jax.random.split(jax.random.fold_in(key, 41), blocks * N_ROWS)

    def choose(segment_key):
        return jax.random.permutation(segment_key, segment)[:share].astype(jnp.int32)
    chosen = jax.vmap(choose)(keys).reshape(blocks, N_ROWS, share)
    block_offsets = jnp.arange(blocks, dtype=jnp.int32)[:, None, None] * PAD_DEV
    segment_offsets = jnp.arange(N_ROWS, dtype=jnp.int32)[None, :, None] * segment
    return (chosen + block_offsets + segment_offsets).reshape(KEPT).astype(jnp.int32)


def setup_inputs(seed: int = 0) -> dict:
    seeds = jax.random.split(jax.random.key(seed), 5)
    return {
        "hidden_acts": draw_hidden_acts(jax.random.fold_in(seeds[4], 71), 0),
        "out_grads": draw_out_grads(jax.random.fold_in(seeds[4], 71), 0),
        "row_signs": draw_row_signs(jax.random.fold_in(seeds[4], 71), 0),
        "kept_index": draw_kept_index(jax.random.fold_in(seeds[4], 71), 0),
    }


epsilon = 1e-06

def sylvester(length):
    indices = jnp.arange(length, dtype=jnp.int32)
    intersection = indices[:, None] & indices[None, :]
    parity = jnp.zeros_like(intersection)
    for bit_level in range(length.bit_length() - 1):
        parity = parity ^ intersection >> bit_level & 1
    return (1 - 2 * parity).astype(jnp.float32)

def reference(hidden_acts, out_grads, row_signs, kept_index):
    pad_rows = PADDED // N_ROWS
    own_rows = FF // N_ROWS
    width = D // N_COLS
    inner_table = sylvester(pad_rows)
    outer_table = sylvester(N_ROWS)
    sign_column = row_signs[:, None].astype(jnp.float32)
    results = []
    for example in range(EXAMPLES):
        squares_all = jnp.zeros((), jnp.float32)
        columns = []
        for block_index in range(N_COLS):
            grads_block = out_grads[example][:, block_index * width:(block_index + 1) * width]
            gradient = jnp.dot(hidden_acts[example], grads_block, preferred_element_type=jnp.float32)
            squares_all = squares_all + jnp.sum(gradient * gradient)
            signed = gradient * sign_column
            stacked = signed.reshape(N_ROWS, own_rows, width)
            stacked = jnp.pad(stacked, ((0, 0), (0, pad_rows - own_rows), (0, 0)))
            inner_mixed = jnp.einsum('ij,bjc->bic', inner_table, stacked, precision=lax.Precision.HIGHEST)
            mixed_rows = jnp.einsum('ab,bic->aic', outer_table, inner_mixed, precision=lax.Precision.HIGHEST)
            mixed_rows = mixed_rows.reshape(PADDED, width)
            columns.append(jnp.take(mixed_rows, kept_index, axis=0))
        inv_norm = 1.0 / jnp.sqrt(squares_all / D + epsilon)
        results.append(jnp.concatenate(columns, axis=1) * inv_norm)
    return jnp.stack(results)
```

```python
import functools

import jax
import jax.numpy as jnp
from jax import lax
from jax.experimental import pallas as pl
from jax.experimental.pallas import tpu as pltpu
from jax.sharding import PartitionSpec as P

D = 5120
PADDED = 32768
LANES = 128

epsilon = 1e-06


def exchange(value, axis, mask):
    pairs = [(source, source ^ mask) for source in range(lax.axis_size(axis))]
    return lax.ppermute(value, axis, pairs)


def split(value):
    high = lax.reduce_precision(value, 8, 7)
    return high.astype(jnp.bfloat16), (value - high).astype(jnp.bfloat16)


def mix_segments(block, segments):
    rows, tokens = block.shape
    parts = [block.reshape(segments, rows // segments, tokens)[s] for s in range(segments)]
    return jnp.stack(butterfly(parts))


def butterfly(parts):
    segments = len(parts)
    step = 1
    while step < segments:
        parts = [
            parts[s ^ step] - parts[s] if s & step else parts[s] + parts[s ^ step]
            for s in range(segments)
        ]
        step *= 2
    return parts


def table(kept, length):
    column = jnp.arange(length, dtype=jnp.int32)
    parity = lax.population_count((kept & (length - 1))[..., None] & column) & 1
    return (1 - 2 * parity).astype(jnp.bfloat16)


def pick(tables, mixed):
    product = lambda part: jnp.einsum(
        "skj,sjt->skt", tables, part, preferred_element_type=jnp.float32
    )
    high, low = split(mixed)
    return product(high) + product(low)


def operands(own, outer, side, inner):
    flipped = side * own
    return (
        side * outer + own,
        outer - flipped,
        jnp.where(inner, side * outer - own, own),
        flipped,
    )


def pick_kernel(segments, flags_ref, own_ref, outer_ref, table_ref, far_ref, here_ref, near_ref, padded, halves):
    own_rows, tokens = own_ref.shape
    length = padded.shape[1] // segments
    rows = min(length, 32)
    padded[0, :own_rows] = own_ref[...]
    padded[1, :own_rows] = outer_ref[...]
    if own_rows < padded.shape[1]:
        rest = jnp.zeros((padded.shape[1] - own_rows, tokens), jnp.float32)
        padded[0, own_rows:] = rest
        padded[1, own_rows:] = rest
    side = flags_ref[0]
    inner = flags_ref[1]

    @pl.loop(0, length // rows)
    def _(step):
        start = pl.multiple_of(step * rows, rows)
        mixed = [
            butterfly([padded[i, pl.ds(s * length + start, rows), :] for s in range(segments)])
            for i in range(2)
        ]
        for s in range(segments):
            own, outer = mixed[0][s], mixed[1][s]
            flipped = side * own
            here = inner * (side * outer) + (1.0 - 2.0 * inner) * own
            for k, value in enumerate((side * outer + own, outer - flipped, here, flipped)):
                high = value.astype(jnp.bfloat16)
                halves[k, s, pl.ds(start, rows), :tokens] = high
                halves[k, s, pl.ds(start, rows), tokens:] = (
                    value - high.astype(jnp.float32)
                ).astype(jnp.bfloat16)

    @pl.loop(0, segments)
    def _(s):
        for k, out in enumerate((far_ref.at[0], far_ref.at[1], here_ref, near_ref)):
            both = jnp.dot(table_ref[k, s], halves[k, s], preferred_element_type=jnp.float32)
            out[s] = both[:, :tokens] + both[:, tokens:]


def pick_all(tables, own, outer, side, inner, pad_rows):
    _, segments, kept, length = tables.shape
    own_rows, tokens = own.shape
    if length % 32 or kept % 16 or segments > 8:
        padding = ((0, pad_rows - own_rows), (0, 0))
        mixed = mix_segments(jnp.pad(own, padding), segments)
        mixed_outer = mix_segments(jnp.pad(outer, padding), segments)
        found = [pick(t, v) for t, v in zip(tables, operands(mixed, mixed_outer, side, inner))]
        return jnp.stack(found[:2]), found[2], found[3]
    flags = jnp.stack([side, inner.astype(jnp.float32)])
    vmem = pl.BlockSpec(memory_space=pltpu.VMEM)
    shape = lambda *lead: jax.ShapeDtypeStruct((*lead, segments, kept, tokens), jnp.float32)
    return pl.pallas_call(
        functools.partial(pick_kernel, segments),
        out_shape=(shape(2), shape(), shape()),
        in_specs=[pl.BlockSpec(memory_space=pltpu.SMEM), vmem, vmem, vmem],
        out_specs=(vmem, vmem, vmem),
        scratch_shapes=[
            pltpu.VMEM((2, pad_rows, tokens), jnp.float32),
            pltpu.VMEM((4, segments, length, 2 * tokens), jnp.bfloat16),
        ],
        compiler_params=pltpu.CompilerParams(vmem_limit_bytes=40 * 2**20),
        cost_estimate=pl.CostEstimate(
            flops=16 * segments * kept * length * tokens,
            bytes_accessed=2 * tables.size + 8 * own.size + 16 * segments * kept * tokens,
            transcendentals=0,
        ),
    )(flags, own, outer, tables)


def add_kernel(slots, first, last, places_ref, *refs):
    kept_refs, grads_refs = refs[:slots], refs[slots : 2 * slots]
    out_ref = refs[-1]
    kept = [ref[...] for ref in kept_refs]
    high = [value.astype(jnp.bfloat16) for value in kept]
    low = [(v - h.astype(jnp.float32)).astype(jnp.bfloat16) for v, h in zip(kept, high)]
    grads = jnp.concatenate([ref[...] for ref in grads_refs], axis=0)
    total = jnp.dot(jnp.concatenate(high, axis=1), grads, preferred_element_type=jnp.float32)
    total += jnp.dot(jnp.concatenate(low, axis=1), grads, preferred_element_type=jnp.float32)
    if not first:
        total += refs[2 * slots][...]
    if last:
        total *= refs[2 * slots + (0 if first else 1)][0]
    out_ref[...] = total


def add_products(total, kept, out_grads, places, scale):
    slots = len(kept)
    keep, chunk = kept[0].shape
    width = out_grads.shape[1]
    tile = min(256, keep)
    slab = pl.BlockSpec((tile, width), lambda i, places: (i, 0))
    grads_spec = lambda slot: pl.BlockSpec((chunk, width), lambda i, places: (places[slot], 0))
    in_specs = [pl.BlockSpec((tile, chunk), lambda i, places: (i, 0))] * slots
    in_specs += [grads_spec(slot) for slot in range(slots)]
    operands_ = list(kept) + [out_grads] * slots
    aliases = {}
    if total is not None:
        aliases = {1 + len(operands_): 0}
        in_specs.append(slab)
        operands_.append(total)
    if scale is not None:
        in_specs.append(pl.BlockSpec(memory_space=pltpu.SMEM))
        operands_.append(scale.reshape(1))
    return pl.pallas_call(
        functools.partial(add_kernel, slots, total is None, scale is not None),
        out_shape=jax.ShapeDtypeStruct((keep, width), jnp.float32),
        grid_spec=pltpu.PrefetchScalarGridSpec(
            num_scalar_prefetch=1,
            grid=(keep // tile,),
            in_specs=in_specs,
            out_specs=slab,
        ),
        input_output_aliases=aliases,
        compiler_params=pltpu.CompilerParams(vmem_limit_bytes=40 * 2**20),
        cost_estimate=pl.CostEstimate(
            flops=4 * slots * keep * chunk * width,
            bytes_accessed=8 * keep * width + 4 * slots * keep * chunk,
            transcendentals=0,
        ),
    )(places, *operands_)


def after(value, earlier):
    if earlier is None:
        return value
    return lax.optimization_barrier((value, earlier))[0]


def local(hidden_acts, out_grads, row_signs, kept_index):
    row_devices = lax.axis_size("rows")
    col_devices = lax.axis_size("cols")
    pad_rows = PADDED // row_devices
    examples, own_rows, tokens = hidden_acts.shape
    keep = kept_index.shape[0]
    length = pad_rows // row_devices
    position = lax.axis_index("rows")
    column = lax.axis_index("cols")
    low = row_devices // 4
    line = position // low
    offset = position % low
    inner = (line == 1) | (line == 2)
    left = line < 2

    kept_all = lax.all_gather(kept_index, "rows", axis=0)

    def kept_of(group):
        whole = lax.dynamic_index_in_dim(kept_all, group * low + offset, 0, keepdims=False)
        return whole.reshape(row_devices, keep // row_devices)

    own_kept = kept_index.reshape(row_devices, keep // row_devices)
    tables = table(
        jnp.stack(
            [
                kept_of(jnp.where(left, 2, 1)),
                kept_of(jnp.where(left, 3, 0)),
                own_kept,
                kept_of(jnp.where(left, 0, 3)),
            ]
        ),
        length,
    )

    line_pairs = lambda pairs: [(s * low + o, d * low + o) for s, d in pairs for o in range(low)]
    to_inner = line_pairs([(0, 1), (3, 2)])
    across = line_pairs([(1, 2), (2, 1)])
    to_outer = line_pairs([(1, 0), (2, 3)])

    share = tokens // col_devices
    chunk = min(LANES, share)
    signs = row_signs.astype(jnp.float32)[:, None]
    side = jnp.where(left, 1.0, -1.0).astype(jnp.float32)
    block = share // chunk
    results = []
    for example in range(examples):
        grads = out_grads[example]
        gradient = jnp.dot(hidden_acts[example], grads, preferred_element_type=jnp.float32)
        squares = lax.psum(jnp.sum(gradient * gradient), ("rows", "cols"))
        inv_norm = lax.rsqrt(squares / D + epsilon)
        total = None
        done = {}

        def send(value, name, move):
            arrived = move(after(value, done.get(name)))
            done[name] = arrived
            return arrived

        for number in range(block):
            acts = lax.dynamic_slice_in_dim(
                hidden_acts[example], column * share + number * chunk, chunk, 1
            )
            own = acts.astype(jnp.float32) * signs
            mask = 1
            while mask < low:
                other = send(own, ("mix", mask), lambda v: exchange(v, "rows", mask))
                own = jnp.where((position & mask) != 0, other - own, own + other)
                mask *= 2
            outer = send(own, "inner", lambda v: lax.ppermute(v, "rows", to_inner))
            far, here, near = pick_all(tables, own, outer, side, inner, pad_rows)
            arrived = send(far, "across", lambda v: lax.ppermute(v, "rows", across))
            last = send(
                arrived[1] + near, "outer", lambda v: lax.ppermute(v, "rows", to_outer)
            )
            kept = here + jnp.where(inner, arrived[0], last)
            slots = [kept.reshape(keep, chunk)]
            order = [0]
            mask = col_devices // 2
            while mask:
                slots += [
                    send(v, ("cols", mask), lambda v: exchange(v, "cols", mask)) for v in slots
                ]
                order += [slot ^ mask for slot in order]
                mask //= 2
            places = jnp.stack([(column ^ slot) * block + number for slot in order])
            scale = inv_norm if number == block - 1 else None
            total = add_products(total, slots, grads, places, scale)
        results.append(total)
    return jnp.stack(results)


def solution(mesh):
    return jax.shard_map(
        local,
        mesh=mesh,
        in_specs=(P(None, "rows", None), P(None, None, "cols"), P("rows"), P("rows")),
        out_specs=P(None, "rows", "cols"),
        check_vma=False,
    )
```

```python
import functools

import jax
import jax.numpy as jnp
from jax import lax
from jax.experimental import pallas as pl
from jax.experimental.pallas import tpu as pltpu
from jax.sharding import PartitionSpec as P

D = 5120
PADDED = 32768
LANES = 128

epsilon = 1e-06


def exchange(value, axis, mask):
    pairs = [(source, source ^ mask) for source in range(lax.axis_size(axis))]
    return lax.ppermute(value, axis, pairs)


def split(value):
    high = lax.reduce_precision(value, 8, 7)
    return high.astype(jnp.bfloat16), (value - high).astype(jnp.bfloat16)


def mix_segments(block, segments):
    rows, tokens = block.shape
    parts = [block.reshape(segments, rows // segments, tokens)[s] for s in range(segments)]
    return jnp.stack(butterfly(parts))


def butterfly(parts):
    segments = len(parts)
    step = 1
    while step < segments:
        parts = [
            parts[s ^ step] - parts[s] if s & step else parts[s] + parts[s ^ step]
            for s in range(segments)
        ]
        step *= 2
    return parts


def table(kept, length):
    column = jnp.arange(length, dtype=jnp.int32)
    parity = lax.population_count((kept & (length - 1))[..., None] & column) & 1
    return (1 - 2 * parity).astype(jnp.bfloat16)


def pick(tables, mixed):
    product = lambda part: jnp.einsum(
        "skj,sjt->skt", tables, part, preferred_element_type=jnp.float32
    )
    high, low = split(mixed)
    return product(high) + product(low)


def operands(own, outer, side, inner):
    flipped = side * own
    return (
        side * outer + own,
        outer - flipped,
        jnp.where(inner, side * outer - own, own),
        flipped,
    )


def pick_kernel(segments, flags_ref, own_ref, outer_ref, table_ref, far_ref, here_ref, near_ref, padded, halves):
    own_rows, tokens = own_ref.shape
    length = padded.shape[1] // segments
    rows = min(length, 32)
    padded[0, :own_rows] = own_ref[...]
    padded[1, :own_rows] = outer_ref[...]
    if own_rows < padded.shape[1]:
        rest = jnp.zeros((padded.shape[1] - own_rows, tokens), jnp.float32)
        padded[0, own_rows:] = rest
        padded[1, own_rows:] = rest
    side = flags_ref[0]
    inner = flags_ref[1]

    @pl.loop(0, length // rows)
    def _(step):
        start = pl.multiple_of(step * rows, rows)
        mixed = [
            butterfly([padded[i, pl.ds(s * length + start, rows), :] for s in range(segments)])
            for i in range(2)
        ]
        for s in range(segments):
            own, outer = mixed[0][s], mixed[1][s]
            flipped = side * own
            here = inner * (side * outer) + (1.0 - 2.0 * inner) * own
            for k, value in enumerate((side * outer + own, outer - flipped, here, flipped)):
                high = value.astype(jnp.bfloat16)
                halves[k, s, pl.ds(start, rows), :tokens] = high
                halves[k, s, pl.ds(start, rows), tokens:] = (
                    value - high.astype(jnp.float32)
                ).astype(jnp.bfloat16)

    @pl.loop(0, segments)
    def _(s):
        for k, out in enumerate((far_ref.at[0], far_ref.at[1], here_ref, near_ref)):
            both = jnp.dot(table_ref[k, s], halves[k, s], preferred_element_type=jnp.float32)
            out[s] = both[:, :tokens] + both[:, tokens:]


def pick_all(tables, own, outer, side, inner, pad_rows):
    _, segments, kept, length = tables.shape
    own_rows, tokens = own.shape
    if length % 32 or kept % 16 or segments > 8:
        padding = ((0, pad_rows - own_rows), (0, 0))
        mixed = mix_segments(jnp.pad(own, padding), segments)
        mixed_outer = mix_segments(jnp.pad(outer, padding), segments)
        found = [pick(t, v) for t, v in zip(tables, operands(mixed, mixed_outer, side, inner))]
        return jnp.stack(found[:2]), found[2], found[3]
    flags = jnp.stack([side, inner.astype(jnp.float32)])
    vmem = pl.BlockSpec(memory_space=pltpu.VMEM)
    shape = lambda *lead: jax.ShapeDtypeStruct((*lead, segments, kept, tokens), jnp.float32)
    return pl.pallas_call(
        functools.partial(pick_kernel, segments),
        out_shape=(shape(2), shape(), shape()),
        in_specs=[pl.BlockSpec(memory_space=pltpu.SMEM), vmem, vmem, vmem],
        out_specs=(vmem, vmem, vmem),
        scratch_shapes=[
            pltpu.VMEM((2, pad_rows, tokens), jnp.float32),
            pltpu.VMEM((4, segments, length, 2 * tokens), jnp.bfloat16),
        ],
        compiler_params=pltpu.CompilerParams(vmem_limit_bytes=40 * 2**20),
        cost_estimate=pl.CostEstimate(
            flops=16 * segments * kept * length * tokens,
            bytes_accessed=2 * tables.size + 8 * own.size + 16 * segments * kept * tokens,
            transcendentals=0,
        ),
    )(flags, own, outer, tables)


def add_kernel(slots, first, last, places_ref, *refs):
    kept_refs, grads_refs = refs[:slots], refs[slots : 2 * slots]
    out_ref = refs[-1]
    kept = [ref[...] for ref in kept_refs]
    high = [value.astype(jnp.bfloat16) for value in kept]
    low = [(v - h.astype(jnp.float32)).astype(jnp.bfloat16) for v, h in zip(kept, high)]
    grads = jnp.concatenate([ref[...] for ref in grads_refs], axis=0)
    total = jnp.dot(jnp.concatenate(high, axis=1), grads, preferred_element_type=jnp.float32)
    total += jnp.dot(jnp.concatenate(low, axis=1), grads, preferred_element_type=jnp.float32)
    if not first:
        total += refs[2 * slots][...]
    if last:
        total *= refs[2 * slots + (0 if first else 1)][0]
    out_ref[...] = total


def add_products(total, kept, out_grads, places, scale):
    slots = len(kept)
    keep, chunk = kept[0].shape
    width = out_grads.shape[1]
    tile = min(256, keep)
    slab = pl.BlockSpec((tile, width), lambda i, places: (i, 0))
    grads_spec = lambda slot: pl.BlockSpec((chunk, width), lambda i, places: (places[slot], 0))
    in_specs = [pl.BlockSpec((tile, chunk), lambda i, places: (i, 0))] * slots
    in_specs += [grads_spec(slot) for slot in range(slots)]
    operands_ = list(kept) + [out_grads] * slots
    aliases = {}
    if total is not None:
        aliases = {1 + len(operands_): 0}
        in_specs.append(slab)
        operands_.append(total)
    if scale is not None:
        in_specs.append(pl.BlockSpec(memory_space=pltpu.SMEM))
        operands_.append(scale.reshape(1))
    return pl.pallas_call(
        functools.partial(add_kernel, slots, total is None, scale is not None),
        out_shape=jax.ShapeDtypeStruct((keep, width), jnp.float32),
        grid_spec=pltpu.PrefetchScalarGridSpec(
            num_scalar_prefetch=1,
            grid=(keep // tile,),
            in_specs=in_specs,
            out_specs=slab,
        ),
        input_output_aliases=aliases,
        compiler_params=pltpu.CompilerParams(vmem_limit_bytes=40 * 2**20),
        cost_estimate=pl.CostEstimate(
            flops=4 * slots * keep * chunk * width,
            bytes_accessed=8 * keep * width + 4 * slots * keep * chunk,
            transcendentals=0,
        ),
    )(places, *operands_)


def after(value, earlier):
    if earlier is None:
        return value
    return lax.optimization_barrier((value, earlier))[0]


def local(hidden_acts, out_grads, row_signs, kept_index):
    row_devices = lax.axis_size("rows")
    col_devices = lax.axis_size("cols")
    pad_rows = PADDED // row_devices
    examples, own_rows, tokens = hidden_acts.shape
    keep = kept_index.shape[0]
    length = pad_rows // row_devices
    position = lax.axis_index("rows")
    column = lax.axis_index("cols")
    low = row_devices // 4
    line = position // low
    offset = position % low
    inner = (line == 1) | (line == 2)
    left = line < 2

    kept_of = lambda step: exchange(kept_index, "rows", step * low).reshape(
        row_devices, keep // row_devices
    )
    own_kept = kept_index.reshape(row_devices, keep // row_devices)
    tables = table(
        jnp.stack(
            [
                kept_of(3),
                kept_of(2),
                own_kept,
                kept_of(1),
            ]
        ),
        length,
    )

    line_pairs = lambda pairs: [(s * low + o, d * low + o) for s, d in pairs for o in range(low)]
    to_inner = line_pairs([(0, 1), (3, 2)])
    across = line_pairs([(1, 2), (2, 1)])
    to_outer = line_pairs([(1, 0), (2, 3)])

    share = tokens // col_devices
    chunk = min(LANES, share)
    signs = row_signs.astype(jnp.float32)[:, None]
    side = jnp.where(left, 1.0, -1.0).astype(jnp.float32)
    block = share // chunk
    results = []
    for example in range(examples):
        grads = out_grads[example]
        gradient = jnp.dot(hidden_acts[example], grads, preferred_element_type=jnp.float32)
        squares = jnp.sum(gradient * gradient).reshape(1)
        part = squares
        for axis, size in (("rows", row_devices), ("cols", col_devices)):
            mask = 1
            while mask < size:
                squares = squares + exchange(squares, axis, mask)
                mask *= 2
        inv_norm = lax.rsqrt(squares / D + epsilon)
        total = None
        done = {}

        def send(value, name, move):
            arrived = move(after(value, done.get(name)))
            done[name] = arrived
            return arrived

        def mix(number, ready):
            acts = lax.dynamic_slice_in_dim(
                hidden_acts[example], column * share + number * chunk, chunk, 1
            )
            own = after(acts.astype(jnp.float32) * signs, ready)
            mask = 1
            while mask < low:
                other = send(own, ("mix", mask), lambda v: exchange(v, "rows", mask))
                if mask * 2 < low:
                    own = jnp.where((position & mask) != 0, other - own, own + other)
                    mask *= 2
                    continue
                upper = (position & mask) != 0
                return lambda v: jnp.where(upper, v[0] - v[1], v[1] + v[0]), (other, own)
            return lambda v: v[1], (own, own)

        join, pair = mix(0, None)
        pair, _ = lax.optimization_barrier((pair, part))
        own = join(pair)
        across_sums = []
        for number in range(block):
            outer = lax.ppermute(own, "rows", to_inner)
            if number + 1 < block:
                join, pair = mix(number + 1, own)
                waits = [tables] if number == 0 else []
                if number >= 2:
                    waits.append(across_sums[number - 2])
                if number == block - 2:
                    waits.append(squares)
                pair, outer, own, *_ = lax.optimization_barrier((pair, outer, own, *waits))
                following = join(pair)
            far, here, near = pick_all(tables, own, outer, side, inner, pad_rows)
            arrived = send(far, "across", lambda v: lax.ppermute(v, "rows", across))
            across_sums.append(arrived)
            last = send(
                arrived[1] + near, "outer", lambda v: lax.ppermute(v, "rows", to_outer)
            )
            kept = here + jnp.where(inner, arrived[0], last)
            slots = [kept.reshape(keep, chunk)]
            order = [0]
            mask = col_devices // 2
            while mask:
                sent = [after(v, total) for v in slots[1:]]
                slots += [
                    send(v, ("cols", mask), lambda v: exchange(v, "cols", mask))
                    for v in [slots[0], *sent]
                ]
                order += [slot ^ mask for slot in order]
                mask //= 2
            places = jnp.stack([(column ^ slot) * block + number for slot in order])
            scale = inv_norm if number == block - 1 else None
            total = add_products(total, slots, grads, places, scale)
            if number + 1 < block:
                own = following
        results.append(total)
    return jnp.stack(results)


def solution(mesh):
    return jax.shard_map(
        local,
        mesh=mesh,
        in_specs=(P(None, "rows", None), P(None, None, "cols"), P("rows"), P("rows")),
        out_specs=P(None, "rows", "cols"),
        check_vma=False,
    )
```
